512 devices in a mesh: wide: 64 (over x, z_hi, y), narrow: 8 (over z_lo, core).
Axes of the slice: x: 4, y: 8, z: 8 (z_hi: 2, z_lo: 4; z = z_hi * 4 + z_lo), core: 2. Of those that a mesh axis runs over, the one named last changes fastest.
Arguments:
- amplitudes: float32 [1024, 16384], P('wide', 'narrow'), may hold values from -6 to 6
- integrals: float32 [16384, 16384], P('narrow', 'wide'), may hold values from -0.125 to 0.125
- residual_in: float32 [1024, 16384], P('narrow', 'wide'), may hold values from -6 to 6
- row_irrep: int32 [1024], P('wide'), may hold values from 0 to 7
- cd_sizes: int32 [8], replicated, may hold values from 1 to 4096, 16384 in all
Outputs:
- ladder_residual: float32 [1024, 16384], P('narrow', 'wide')
The draws below stay inside these ranges and needn't reach their ends.
Inputs may be any that keep to these rules, and one draw needn't show every extreme that they name: `cd_sizes`: sums to 16384; the largest is exactly 4096.
All inputs are finite; a program needn't handle non-finite values.
Results may differ from the reference program's by a relative error of at most 0.00005.
Values sent between devices are 32-bit elements; how exact they have to be, the bound alone decides.
A program may use at most 64 MiB of HBM per device.

```python
import math
import jax
import jax.numpy as jnp
import numpy as np
from jax import lax

NIRREP = 8
KN_DEV = 2048
ROWS = 1024
K = 16384
M = 16384
N_NARROW = 8


def touch_ends(result, rng, least, top_value):
    extent = result.shape
    index_at = [jax.random.randint(jax.random.fold_in(rng, axis), (), 0, extent[axis]) for axis in range(len(extent))]
    result = result.at[tuple(index_at)].set(least)
    longest = extent.index(max(extent))
    index_at[longest] = (index_at[longest] + 1) % extent[longest]
    return result.at[tuple(index_at)].set(top_value)


def levels(own_key, shape, pieces, least, top_value):
    gain, own = 1.0, jax.random.fold_in(own_key, 6)
    for dim, blocks in pieces:
        heights = jnp.exp(jax.random.uniform(jax.random.fold_in(own, dim), (blocks,), jnp.float32, least / len(pieces), top_value / len(pieces)))
        gain = gain * jnp.repeat(heights, shape[dim] // blocks).reshape([-1 if axis == dim else 1 for axis in range(len(shape))])
    return gain


def profile(number_of, total, most, lean):
    loads = [(1 << 20) // math.isqrt(grade ** lean) + 1 for grade in range(2, number_of + 1)]
    spare, holding = total - most - (number_of - 1), [1] * (number_of - 1)
    while spare > 0:
        candidates = [i for i in range(number_of - 1) if holding[i] < most]
        whole, left = sum([loads[i] for i in candidates]), spare
        for i in candidates:
            addition = min(most - holding[i], max(1, left * loads[i] // whole), spare)
            holding[i] = holding[i] + addition
            spare = spare - addition
    return np.array([most] + holding)


def ragged(stream_key, amount, total, bound, slope):
    if amount == 2:
        one = jax.random.randint(stream_key, (), max(1, total - bound), min(bound, total - 1) + 1)
        return jnp.stack([one, total - one])
    sizes = jnp.asarray(profile(amount, total, bound, slope), jnp.int32)
    pairs = (amount - 1) // 2
    source_of, taker = sizes[1:1 + 2 * pairs:2], sizes[2:2 + 2 * pairs:2]
    room = jnp.minimum(source_of - 1, bound - taker)
    shifted = jax.random.randint(jax.random.fold_in(stream_key, 1), (pairs,), 0, 1 << 20) % (room + 1)
    sizes = sizes.at[1:1 + 2 * pairs:2].set(source_of - shifted).at[2:2 + 2 * pairs:2].set(taker + shifted)
    return sizes[jax.random.permutation(jax.random.fold_in(stream_key, 2), amount)]


def scatter_about(key, shape, width, reach, cuts=(), kind=jnp.bfloat16):
    gain = levels(key, shape, cuts, -0.22, 0.18) if cuts else 1.0
    array = jax.random.normal(key, shape, jnp.float32) * width * gain
    return jnp.minimum(jnp.maximum(array, -reach), reach).astype(kind)


def setup_inputs(seed: int = 0) -> dict:
    streams_of = jax.random.split(jax.random.key(seed), 6)
    return {
        "amplitudes": scatter_about(streams_of[0], (ROWS, K), 1.0, 6.0, ((0, 64), (1, 8)), jnp.float32),
        "integrals": scatter_about(streams_of[1], (K, M), (K // NIRREP) ** -0.5, 0.125, ((0, 8), (1, 64)), jnp.float32),
        "residual_in": scatter_about(streams_of[2], (ROWS, M), 1.0, 6.0, ((0, 8), (1, 64)), jnp.float32),
        "row_irrep": touch_ends(jax.random.randint(streams_of[3], (ROWS,), 0, NIRREP), jax.random.fold_in(streams_of[3], 1), 0, NIRREP - 1).astype(jnp.int32),
        "cd_sizes": ragged(streams_of[4], NIRREP, K, K // 4, 2).astype(jnp.int32),
    }


def reference(amplitudes, integrals, residual_in, row_irrep, cd_sizes):
    total = KN_DEV * N_NARROW
    ends = jnp.cumsum(cd_sizes).astype(jnp.int32)
    column = jnp.arange(total, dtype=jnp.int32)
    col_irrep = jnp.sum((column[:, None] >= ends[None, :]).astype(jnp.int32), axis=1)
    masked = jnp.where(row_irrep[:, None] == col_irrep[None, :], amplitudes, jnp.zeros((), amplitudes.dtype))
    ladder = jnp.dot(masked, integrals, precision=lax.Precision.HIGHEST, preferred_element_type=jnp.float32)
    return residual_in + 0.5 * ladder
```

```python
import functools

import jax
import jax.numpy as jnp
from jax import lax
from jax.experimental import pallas as pl
from jax.experimental.pallas import tpu as pltpu
from jax.sharding import PartitionSpec as P

MESH = pl.DeviceIdType.MESH
F32 = jnp.float32
BF16 = jnp.bfloat16

NX, NZH, NY, NZL, NC = 4, 2, 8, 4, 2
RW = 16
RB = RW * NY
CH = 256
AB = 256
SLOTS = 32
CAP = SLOTS - 1
HALF = SLOTS // 2
NIRR = 8


def split(value):
    high = value.astype(BF16)
    return high, (value - high.astype(F32)).astype(BF16)


def dot(a, b):
    return jnp.dot(a, b, preferred_element_type=F32)


def kernel(
    a_ref, int_ref, res_ref, irr_ref, sizes_ref, off_ref,
    out_ref, cnt_ref,
    int_hi, int_lo, ci_ref, irr_row, raw, raw_irr, qbuf, pbuf, sel, irr_col, ranks, acc, pair, zbuf,
    raw_s, raw_r, ri_s, ri_r, qy_s, qy_r, qx_s, qx_r, py_s, py_r, px_s, px_r, pair_s, pair_r, z_s, z_r,
):
    w, n = lax.axis_index("wide"), lax.axis_index("narrow")
    x, zh, y = w // (NZH * NY), (w // NY) % NZH, w % NY
    zl, c = n // NC, n % NC

    def dev(x_, zh_, y_, zl_, c_):
        return (x_ * (NZH * NY) + zh_ * NY + y_, zl_ * NC + c_)

    ymod = lambda k: lax.rem(y + (k + NY), NY)
    xmod = lambda k: lax.rem(x + (k + NX), NX)
    partner = dev(x, zh, y, zl, 1 - c)
    up, down = dev(x, zh, ymod(1), zl, c), dev(x, zh, ymod(-1), zl, c)
    y_peers = [dev(x, zh, ymod(k), zl, c) for k in range(1, NY)]
    o_peers = [dev(x, 1 - zh, ymod(k), zl, c) for k in range(NY)]
    x_peers = [dev(xmod(k), zh, y, zl, c) for k in range(1, NX)]
    z_peers = [dev(x, zh, y, lax.rem(zl + k, NZL), c) for k in range(1, NZL)]

    barrier = pltpu.get_barrier_semaphore()
    everyone = y_peers + o_peers + x_peers + z_peers + [partner]
    for peer in everyone:
        pl.semaphore_signal(barrier, inc=1, device_id=peer, device_id_type=MESH)

    lane = lax.broadcasted_iota(jnp.int32, (8, 128), 1)
    row = jnp.zeros((8, 128), F32)
    for r in range(RW):
        row = jnp.where(lane == y * RW + r, irr_ref[r].astype(F32), row)
    irr_row[...] = row
    cd = (
        n * (NY * CH)
        + CH * lax.broadcasted_iota(jnp.int32, (NY, CH), 0)
        + lax.broadcasted_iota(jnp.int32, (NY, CH), 1)
    )
    end = jnp.int32(0)
    col = jnp.zeros((NY, CH), F32)
    for i in range(NIRR):
        end = end + sizes_ref[i]
        col = col + jnp.where(cd >= end, 1.0, 0.0)
    ci_ref[...] = col
    off = off_ref[0]

    sends = []

    def send(src, dst, s, r, to):
        copy = pltpu.make_async_remote_copy(
            src_ref=src, dst_ref=dst, send_sem=s, recv_sem=r, device_id=to, device_id_type=MESH
        )
        copy.start()
        return copy

    def arrived(dst, r):
        pltpu.make_async_remote_copy(
            src_ref=dst, dst_ref=dst, send_sem=r, recv_sem=r, device_id=partner, device_id_type=MESH
        ).wait_recv()

    chunk = lambda j: pl.ds(pl.multiple_of(j * CH, CH), CH)

    def split_integrals(j, _):
        high, low = split(int_ref[chunk(j), :])
        int_hi[j] = high
        int_lo[j] = low
        return 0

    pl.semaphore_wait(barrier, len(everyone))

    for k in range(1, NY):
        to = y_peers[k - 1]
        sends.append(send(irr_row.at[pl.ds(0, 1)], raw_irr.at[0, pl.ds(y, 1)], ri_s.at[0, k], ri_r.at[0, k], to))
        sends.append(send(a_ref.at[:, chunk(ymod(k))], raw.at[0, y], raw_s.at[0, k], raw_r.at[0, k], to))
    for k in range(NY):
        to = o_peers[k]
        sends.append(send(irr_row.at[pl.ds(0, 1)], raw_irr.at[1, pl.ds(y, 1)], ri_s.at[1, k], ri_r.at[1, k], to))
        sends.append(send(a_ref.at[:, chunk(ymod(k))], raw.at[1, y], raw_s.at[1, k], raw_r.at[1, k], to))
    raw[0, y] = a_ref[:, chunk(y)]
    raw_irr[0, pl.ds(y, 1)] = row[0:1]
    lax.fori_loop(0, NY, split_integrals, 0)

    sub_i = lax.broadcasted_iota(jnp.int32, (RB, RB), 0)
    lane_i = lax.broadcasted_iota(jnp.int32, (RB, RB), 1)

    def ranks_of(irr_lane):
        along_lane = jnp.broadcast_to(irr_lane, (RB, RB))
        along_sub = along_lane.T
        same = along_lane == along_sub
        rank_lane = jnp.sum(jnp.where(same & (sub_i < lane_i), 1.0, 0.0), axis=0, keepdims=True)
        rank_sub = jnp.sum(jnp.where(same & (lane_i < sub_i), 1.0, 0.0), axis=1, keepdims=True)
        return along_sub, rank_lane, rank_sub

    def pack(group, dst):
        irr_lane = jnp.sum(raw_irr[group], axis=0, keepdims=True)
        along_sub, rank_lane, _ = ranks_of(irr_lane)
        slot = lax.broadcasted_iota(jnp.int32, (SLOTS, RB), 0).astype(F32)
        pick = jnp.where((rank_lane - off == slot) & (slot < CAP), 1.0, 0.0).astype(BF16)
        here = ci_ref[pl.ds(y, 1), :]
        keep = jnp.concatenate([along_sub, along_sub], axis=1) == here
        masked = jnp.where(keep, raw[group].reshape(RB, CH), 0.0)
        high = masked.astype(BF16)
        rest = masked - high.astype(F32)
        mid, low = split(rest)
        packed = dot(pick, high) + dot(pick, mid) + dot(pick, low)
        last = lax.broadcasted_iota(jnp.int32, (SLOTS, CH), 0) == CAP
        tail = jnp.concatenate([irr_lane, jnp.zeros((1, CH - RB), F32)], axis=1)
        dst[...] = jnp.where(last, jnp.broadcast_to(tail, (SLOTS, CH)), packed)

    def open_block(b, src):
        irr_lane = src[pl.ds(CAP, 1), 0:RB]
        along_sub, rank_lane, rank_sub = ranks_of(irr_lane)
        slot = lax.broadcasted_iota(jnp.int32, (RB, SLOTS), 1).astype(F32)
        sel[b] = jnp.where((rank_sub - off == slot) & (slot < CAP), 1.0, 0.0).astype(BF16)
        irr_col[b] = along_sub
        ranks[pl.ds(b, 1), :] = rank_lane

    def multiply(b, src, j):
        high, low = split(src[...])
        pick = sel[b]
        keep = jnp.concatenate([irr_col[b], irr_col[b]], axis=1) == ci_ref[pl.ds(j, 1), :]
        e_hi = jnp.where(keep, dot(pick, high), 0.0).astype(BF16)
        e_lo = jnp.where(keep, dot(pick, low), 0.0).astype(BF16)
        return dot(e_hi, int_hi[j]) + dot(e_lo, int_hi[j]) + dot(e_hi, int_lo[j])

    for k in range(1, NY):
        arrived(raw_irr.at[0, pl.ds(ymod(-k), 1)], ri_r.at[0, k])
        arrived(raw.at[0, ymod(-k)], raw_r.at[0, k])
    pack(0, qbuf.at[x, y])

    def q_along_x(j, slot):
        for k in (1, 3, 2):
            sends.append(send(qbuf.at[x, j], qbuf.at[x, j], qx_s.at[slot, k], qx_r.at[slot, k], x_peers[k - 1]))

    def part(ref, half):
        return ref if half is None else ref.at[pl.ds(half * HALF, HALF)]

    def q_along_y(j, s, direction):
        half = direction if s == NY // 2 else None
        ref = part(qbuf.at[x, j], half)
        sends.append(send(ref, ref, qy_s.at[direction, s], qy_r.at[direction, s], (up, down)[direction]))

    def p_along_y(j, k, s, direction):
        half = direction if s == NY // 2 else None
        ref = part(pbuf.at[j, xmod(-k)], half)
        sends.append(send(ref, ref, py_s.at[direction, s, k], py_r.at[direction, s, k], (up, down)[direction]))

    def q_step(s):
        for direction, j in ((0, ymod(-s)), (1, ymod(s))):
            arrived(qbuf.at[x, j], qy_r.at[direction, s])
            q_along_y(j, s + 1, direction)
            q_along_x(j, 2 * s - 1 + direction)

    def p_step(s, ks):
        for k in ks:
            for direction, j in ((0, ymod(-s)), (1, ymod(s))):
                arrived(pbuf.at[j, xmod(-k)], py_r.at[direction, s, k])
                p_along_y(j, k, s + 1, direction)

    q_along_y(y, 1, 0)
    q_along_y(y, 1, 1)
    q_along_x(y, 0)

    for k in range(NY):
        arrived(raw_irr.at[1, pl.ds(ymod(-k), 1)], ri_r.at[1, k])
        arrived(raw.at[1, ymod(-k)], raw_r.at[1, k])
    pack(1, pbuf.at[y, x])
    p_along_y(y, 0, 1, 0)
    p_along_y(y, 0, 1, 1)
    for k in (1, 3, 2):
        sends.append(send(pbuf.at[y, x], pbuf.at[y, x], px_s.at[k], px_r.at[k], x_peers[k - 1]))

    q_step(1)
    for k in (1, 3, 2):
        arrived(pbuf.at[y, xmod(-k)], px_r.at[k])
        p_along_y(y, k, 1, 0)
        p_along_y(y, k, 1, 1)
    q_step(2)
    p_step(1, (0, 1, 3, 2))
    for k in range(NX):
        open_block(NX + k, pbuf.at[y, k])

    def p_multiply(j, first=False):
        def one(k, _):
            term = multiply(NX + k, pbuf.at[j, k], j)
            if first:
                acc[NX + k] = term
            else:
                acc[NX + k] += term
            return 0

        lax.fori_loop(0, NX, one, 0)

    p_multiply(y, first=True)
    q_step(3)
    for k in range(1, NX):
        arrived(qbuf.at[xmod(-k), y], qx_r.at[0, k])
    p_step(2, (0, 1, 3, 2))
    for k in range(NX):
        open_block(k, qbuf.at[k, y])
    p_multiply(ymod(-1))
    p_multiply(ymod(1))
    opposite = ymod(NY // 2)
    for direction in (0, 1):
        arrived(part(qbuf.at[x, opposite], direction), qy_r.at[direction, NY // 2])
    q_along_x(opposite, NY - 1)
    p_step(3, (0, 1, 3, 2))
    p_multiply(ymod(-2))
    p_multiply(ymod(2))

    for s in range(1, NY // 2):
        for k in range(1, NX):
            arrived(qbuf.at[xmod(-k), ymod(-s)], qx_r.at[2 * s - 1, k])
            arrived(qbuf.at[xmod(-k), ymod(s)], qx_r.at[2 * s, k])
    for k in range(1, NX):
        arrived(qbuf.at[xmod(-k), opposite], qx_r.at[NY - 1, k])

    def pair_copy(base, d):
        return pltpu.make_async_remote_copy(
            src_ref=acc.at[base + d], dst_ref=pair.at[d], send_sem=pair_s.at[d], recv_sem=pair_r.at[d],
            device_id=partner, device_id_type=MESH,
        )

    def z_copy(base, d):
        slot = lax.rem(zl - d + NZL, NZL)
        return pltpu.make_async_remote_copy(
            src_ref=acc.at[base + d], dst_ref=zbuf.at[slot], send_sem=z_s.at[d], recv_sem=z_r.at[slot],
            device_id=dev(x, zh, y, d, c), device_id_type=MESH,
        )

    def nth(t):
        return jnp.where(zl < NZL // 2, NZL - 1 - t, t)

    def give(base):
        def one(t, _):
            pair_copy(base, nth(t)).start()
            return 0

        lax.fori_loop(0, NZL, one, 0)

    def take(base):
        def one(t, _):
            d = nth(t)
            arrived(pair.at[d], pair_r.at[d])
            acc[base + d] += pair[d]

            @pl.when(d != zl)
            def _():
                z_copy(base, d).start()

            return 0

        lax.fori_loop(0, NZL, one, 0)

    def finish(base):
        total = acc[base + zl]
        for k in range(1, NZL):
            arrived(zbuf.at[k], z_r.at[k])
            total = total + zbuf[k]
        out_ref[...] = res_ref[...] + 0.5 * total

        def one(d, _):
            @pl.when(d != zl)
            def _():
                z_copy(base, d).wait_send()

            return 0

        lax.fori_loop(0, NZL, one, 0)

    keeps_q = c == zh

    def q_multiply(k, _):
        def one(j, _):
            acc[k] += multiply(k, qbuf.at[k, j], j)
            return 0

        acc[k] = multiply(k, qbuf.at[k, 0], 0)
        lax.fori_loop(1, NY, one, 0)
        return 0

    lax.fori_loop(0, NX, q_multiply, 0)

    @pl.when(jnp.logical_not(keeps_q))
    def _():
        give(0)

    @pl.when(keeps_q)
    def _():
        take(0)

    p_multiply(ymod(-3))
    p_multiply(ymod(3))
    for k in (0, 1, 3, 2):
        for direction in (0, 1):
            arrived(part(pbuf.at[opposite, xmod(-k)], direction), py_r.at[direction, NY // 2, k])
    p_multiply(opposite)

    @pl.when(keeps_q)
    def _():
        give(NX)
        finish(0)
        for d in range(NZL):
            pair_copy(NX, d).wait_send()

    @pl.when(jnp.logical_not(keeps_q))
    def _():
        take(NX)
        finish(NX)
        for d in range(NZL):
            pair_copy(0, d).wait_send()

    cnt_ref[0] = jnp.max(ranks[...])
    for copy in sends:
        copy.wait_send()


def one_pass(amplitudes, integrals, start, row_irrep, cd_sizes, off):
    dma = pltpu.SemaphoreType.DMA
    vmem, smem = pl.BlockSpec(memory_space=pltpu.VMEM), pl.BlockSpec(memory_space=pltpu.SMEM)
    return pl.pallas_call(
        kernel,
        out_shape=(jax.ShapeDtypeStruct((RB, AB), F32), jax.ShapeDtypeStruct((1,), F32)),
        in_specs=[vmem, vmem, vmem, smem, smem, smem],
        out_specs=(vmem, smem),
        scratch_shapes=[
            pltpu.VMEM((NY, CH, AB), BF16),
            pltpu.VMEM((NY, CH, AB), BF16),
            pltpu.VMEM((NY, CH), F32),
            pltpu.VMEM((8, RB), F32),
            pltpu.VMEM((2, NY, RW, CH), F32),
            pltpu.VMEM((2, NY, RB), F32),
            pltpu.VMEM((NX, NY, SLOTS, CH), F32),
            pltpu.VMEM((NY, NX, SLOTS, CH), F32),
            pltpu.VMEM((2 * NX, RB, SLOTS), BF16),
            pltpu.VMEM((2 * NX, RB, RB), F32),
            pltpu.VMEM((2 * NX, RB), F32),
            pltpu.VMEM((2 * NX, RB, AB), F32),
            pltpu.VMEM((NZL, RB, AB), F32),
            pltpu.VMEM((NZL, RB, AB), F32),
            dma((2, NY)), dma((2, NY)), dma((2, NY)), dma((2, NY)),
            dma((2, 5)), dma((2, 5)), dma((NY, NX)), dma((NY, NX)),
            dma((2, 5, NX)), dma((2, 5, NX)), dma((NX,)), dma((NX,)),
            dma((NZL,)), dma((NZL,)), dma((NZL,)), dma((NZL,)),
        ],
        compiler_params=pltpu.CompilerParams(
            collective_id=0, has_side_effects=True, vmem_limit_bytes=40 * 2**20
        ),
        name="ladder",
    )(amplitudes, integrals, start, row_irrep, cd_sizes, off)


def body(amplitudes, integrals, residual_in, row_irrep, cd_sizes):
    def run(start, off):
        return one_pass(amplitudes, integrals, start, row_irrep, cd_sizes, off)

    def more(state):
        _, top, off = state
        return top[0] >= off[0]

    def again(state):
        total, _, off = state
        total, top = run(total, off)
        return total, top, off + CAP

    zero = jnp.zeros((1,), F32)
    total, top = run(residual_in, zero)
    return lax.while_loop(more, again, (total, top, zero + CAP))[0]


def solution(mesh):
    in_specs = (P("wide", "narrow"), P("narrow", "wide"), P("narrow", "wide"), P("wide"), P())
    out_specs = P("narrow", "wide")
    return jax.shard_map(body, mesh=mesh, in_specs=in_specs, out_specs=out_specs, check_vma=False)
```

```python
import functools

import jax
import jax.numpy as jnp
from jax import lax
from jax.experimental import pallas as pl
from jax.experimental.pallas import tpu as pltpu
from jax.sharding import PartitionSpec as P

MESH = pl.DeviceIdType.MESH
F32 = jnp.float32
BF16 = jnp.bfloat16

NX, NZH, NY, NZL, NC = 4, 2, 8, 4, 2
RW = 16
RB = RW * NY
CH = 256
AB = 256
SLOTS = 32
CAP = SLOTS - 1
HALF = SLOTS // 2
NIRR = 8


def split(value):
    high = value.astype(BF16)
    return high, (value - high.astype(F32)).astype(BF16)


def dot(a, b):
    return jnp.dot(a, b, preferred_element_type=F32)


def kernel(
    a_hbm, int_hbm, res_hbm, irr_hbm, sizes_hbm, off_hbm,
    out_ref, cnt_ref,
    a_ref, int_ref, res_ref, irr_ref, sizes_ref, off_ref, int3, ci_ref, irr_row, raw, raw_irr, qbuf, pbuf, sel, irr_col, ranks, acc, pair, zbuf,
    in_s, raw_s, raw_r, ri_s, ri_r, qy_s, qy_r, qx_s, qx_r, py_s, py_r, px_s, px_r, zx_s, zx_r,
    pair_s, pair_r, z_s, z_r,
):
    w, n = lax.axis_index("wide"), lax.axis_index("narrow")
    x, zh, y = w // (NZH * NY), (w // NY) % NZH, w % NY
    zl, c = n // NC, n % NC

    def dev(x_, zh_, y_, zl_, c_):
        return (x_ * (NZH * NY) + zh_ * NY + y_, zl_ * NC + c_)

    ymod = lambda k: lax.rem(y + (k + NY), NY)
    xmod = lambda k: lax.rem(x + (k + NX), NX)
    partner = dev(x, zh, y, zl, 1 - c)
    up, down = dev(x, zh, ymod(1), zl, c), dev(x, zh, ymod(-1), zl, c)
    y_peers = [dev(x, zh, ymod(k), zl, c) for k in range(1, NY)]
    across = dev(x, 1 - zh, y, zl, c)
    x_peers = [dev(xmod(k), zh, y, zl, c) for k in range(1, NX)]
    z_peers = [dev(x, zh, y, lax.rem(zl + k, NZL), c) for k in range(1, NZL)]

    barrier = pltpu.get_barrier_semaphore()
    everyone = y_peers + x_peers + z_peers + [partner, across]
    for peer in everyone:
        pl.semaphore_signal(barrier, inc=1, device_id=peer, device_id_type=MESH)

    loads = [
        pltpu.make_async_copy(src, dst, in_s.at[i])
        for i, (src, dst) in enumerate((
            (a_hbm, a_ref), (int_hbm, int_ref), (res_hbm, res_ref),
            (irr_hbm, irr_ref), (sizes_hbm, sizes_ref), (off_hbm, off_ref),
        ))
    ]
    for load in loads:
        load.start()
    for load in loads[3:]:
        load.wait()
    lane = lax.broadcasted_iota(jnp.int32, (8, 128), 1)
    row = jnp.zeros((8, 128), F32)
    for r in range(RW):
        row = jnp.where(lane == y * RW + r, irr_ref[r].astype(F32), row)
    irr_row[...] = row
    cd = (
        n * (NY * CH)
        + CH * lax.broadcasted_iota(jnp.int32, (NY, CH), 0)
        + lax.broadcasted_iota(jnp.int32, (NY, CH), 1)
    )
    end = jnp.int32(0)
    col = jnp.zeros((NY, CH), F32)
    for i in range(NIRR):
        end = end + sizes_ref[i]
        col = col + jnp.where(cd >= end, 1.0, 0.0)
    ci_ref[...] = col
    off = off_ref[0]

    def send(src, dst, s, r, to):
        copy = pltpu.make_async_remote_copy(
            src_ref=src, dst_ref=dst, send_sem=s, recv_sem=r, device_id=to, device_id_type=MESH
        )
        copy.start()

    def sent(total, s):
        pltpu.make_async_remote_copy(
            src_ref=total, dst_ref=total, send_sem=s, recv_sem=s, device_id=partner, device_id_type=MESH
        ).wait_send()

    def arrived(dst, r):
        pltpu.make_async_remote_copy(
            src_ref=dst, dst_ref=dst, send_sem=r, recv_sem=r, device_id=partner, device_id_type=MESH
        ).wait_recv()

    chunk = lambda j: pl.ds(pl.multiple_of(j * CH, CH), CH)

    def split_integrals(j, _):
        high, low = split(int_ref[chunk(j), :])
        int3[j, 0:CH] = high
        int3[j, CH:2 * CH] = high
        int3[j, 2 * CH:] = low
        return 0

    loads[0].wait()
    pl.semaphore_wait(barrier, len(everyone))

    for k in (4, 3, 5, 2, 6, 1, 7):
        to = y_peers[k - 1]
        send(irr_row.at[pl.ds(0, 1)], raw_irr.at[pl.ds(y, 1)], ri_s.at[0], ri_r.at[0], to)
        send(a_ref.at[:, chunk(ymod(k))], raw.at[y], raw_s.at[0], raw_r.at[0], to)
    raw[y] = a_ref[:, chunk(y)]
    raw_irr[pl.ds(y, 1), :] = row[0:1]
    loads[1].wait()
    lax.fori_loop(0, NY, split_integrals, 0)

    sub_i = lax.broadcasted_iota(jnp.int32, (RB, RB), 0)
    lane_i = lax.broadcasted_iota(jnp.int32, (RB, RB), 1)

    def ranks_of(irr_lane):
        along_lane = jnp.broadcast_to(irr_lane, (RB, RB))
        along_sub = along_lane.T
        same = along_lane == along_sub
        rank_lane = jnp.sum(jnp.where(same & (sub_i < lane_i), 1.0, 0.0), axis=0, keepdims=True)
        rank_sub = jnp.sum(jnp.where(same & (lane_i < sub_i), 1.0, 0.0), axis=1, keepdims=True)
        return along_sub, rank_lane, rank_sub

    def pack(dst):
        irr_lane = jnp.sum(raw_irr[...], axis=0, keepdims=True)
        along_sub, rank_lane, _ = ranks_of(irr_lane)
        slot = lax.broadcasted_iota(jnp.int32, (SLOTS, RB), 0).astype(F32)
        pick = jnp.where((rank_lane - off == slot) & (slot < CAP), 1.0, 0.0).astype(BF16)
        here = ci_ref[pl.ds(y, 1), :]
        keep = jnp.concatenate([along_sub, along_sub], axis=1) == here
        masked = jnp.where(keep, raw[...].reshape(RB, CH), 0.0)
        high = masked.astype(BF16)
        rest = masked - high.astype(F32)
        mid, low = split(rest)
        packed = dot(pick, high) + dot(pick, mid) + dot(pick, low)
        last = lax.broadcasted_iota(jnp.int32, (SLOTS, CH), 0) == CAP
        tail = jnp.concatenate([irr_lane, jnp.zeros((1, CH - RB), F32)], axis=1)
        dst[...] = jnp.where(last, jnp.broadcast_to(tail, (SLOTS, CH)), packed)

    def open_blocks(g, srcs):
        for k, src in enumerate(srcs):
            irr_lane = src[pl.ds(CAP, 1), 0:RB]
            along_sub, rank_lane, rank_sub = ranks_of(irr_lane)
            slot = lax.broadcasted_iota(jnp.int32, (RB, NX * SLOTS), 1) - k * SLOTS
            pick = (rank_sub - off == slot.astype(F32)) & (slot >= 0) & (slot < CAP)
            sel[g, k * RB:(k + 1) * RB, :] = jnp.where(pick, 1.0, 0.0).astype(BF16)
            irr_col[g, k * RB:(k + 1) * RB, :] = along_sub
            ranks[pl.ds(NX * g + k, 1), :] = rank_lane

    def multiply(g, src, j, first=False):
        high, low = split(src.reshape(NX * SLOTS, CH))
        spread = dot(sel[g], jnp.concatenate([high, low], axis=1))
        keep = jnp.concatenate([irr_col[g], irr_col[g]], axis=1) == ci_ref[pl.ds(j, 1), :]
        e_hi = jnp.where(keep, spread[:, :CH], 0.0).astype(BF16)
        e_lo = jnp.where(keep, spread[:, CH:], 0.0).astype(BF16)
        term = dot(jnp.concatenate([e_hi, e_lo, e_hi], axis=1), int3[j])
        if first:
            acc[g] = term
        else:
            acc[g] += term

    arrived(raw_irr.at[pl.ds(0, NY - 1)], ri_r.at[0])
    arrived(raw.at[pl.ds(0, NY - 1)], raw_r.at[0])
    pack(qbuf.at[x, y])

    def q_along_x(j, slot):
        for k in (1, 3, 2):
            send(qbuf.at[x, j], qbuf.at[x, j], qx_s.at[0], qx_r.at[slot], x_peers[k - 1])

    def part(ref, half):
        return ref if half is None else ref.at[pl.ds(half * HALF, HALF)]

    def p_along_y(j, k, s, direction):
        half = direction if s == NY // 2 else None
        ref = part(pbuf.at[j, xmod(-k)], half)
        send(ref, ref, py_s.at[0], py_r.at[direction, s, k], (up, down)[direction])

    def q_step(k):
        arrived(qbuf.at[x, ymod(-k)], qy_r.at[k])
        q_along_x(ymod(-k), k)

    def p_step(s, ks):
        for k in ks:
            for direction, j in ((0, ymod(-s)), (1, ymod(s))):
                arrived(pbuf.at[j, xmod(-k)], py_r.at[direction, s, k])
                p_along_y(j, k, s + 1, direction)

    send(qbuf.at[x, y], pbuf.at[y, x], zx_s.at[0], zx_r.at[0], across)
    for k in (1, 7, 2, 6, 3, 5, 4):
        send(qbuf.at[x, y], qbuf.at[x, y], qy_s.at[0], qy_r.at[k], y_peers[k - 1])
    q_along_x(y, 0)

    opposite = ymod(NY // 2)

    def q_multiply(slot, first=False):
        j = ymod(-slot)
        arrived(qbuf.at[0, pl.ds(0, NX - 1)], qx_r.at[slot])
        if first:
            open_blocks(0, [qbuf.at[k, j] for k in range(NX)])
        multiply(0, qbuf[:, j], j, first)

    def p_multiply(j, first=False):
        if first:
            open_blocks(1, [pbuf.at[j, k] for k in range(NX)])
        multiply(1, pbuf[j], j, first)

    for k in (1, 7, 2, 6):
        q_step(k)
    arrived(pbuf.at[y, x], zx_r.at[0])
    p_along_y(y, 0, 1, 0)
    p_along_y(y, 0, 1, 1)
    for k in (1, 3, 2):
        send(pbuf.at[y, x], pbuf.at[y, x], px_s.at[0], px_r.at[k], x_peers[k - 1])
    for k in (3, 5, 4):
        q_step(k)
    q_multiply(0, first=True)
    p_step(1, (0,))
    for k in (1, 3, 2):
        arrived(pbuf.at[y, xmod(-k)], px_r.at[k])
        p_along_y(y, k, 1, 0)
        p_along_y(y, k, 1, 1)
    q_multiply(1)
    q_multiply(7)
    p_step(1, (1, 3, 2))
    p_multiply(y, first=True)
    q_multiply(2)
    q_multiply(6)
    p_step(2, (0,))
    q_multiply(3)
    q_multiply(5)
    p_step(2, (1, 3, 2))
    q_multiply(4)

    block = lambda d: pl.ds(pl.multiple_of(d * RB, RB), RB)

    def pair_copy(g, d):
        return pltpu.make_async_remote_copy(
            src_ref=acc.at[g, block(d)], dst_ref=pair.at[d], send_sem=pair_s.at[0], recv_sem=pair_r.at[d],
            device_id=partner, device_id_type=MESH,
        )

    def z_copy(g, d):
        slot = lax.rem(zl - d + NZL, NZL) - 1
        return pltpu.make_async_remote_copy(
            src_ref=acc.at[g, block(d)], dst_ref=zbuf.at[slot], send_sem=z_s.at[0], recv_sem=z_r.at[0],
            device_id=dev(x, zh, y, d, c), device_id_type=MESH,
        )

    def nth(t):
        return jnp.where(zl < NZL // 2, NZL - 1 - t, t)

    def give(g):
        def one(t, _):
            pair_copy(g, nth(t)).start()
            return 0

        lax.fori_loop(0, NZL, one, 0)

    def take(g):
        def one(t, _):
            d = nth(t)
            arrived(pair.at[d], pair_r.at[d])
            acc[g, block(d)] += pair[d]

            @pl.when(d != zl)
            def _():
                z_copy(g, d).start()

            return 0

        lax.fori_loop(0, NZL, one, 0)

    def finish(g):
        total = acc[g, block(zl)]
        arrived(zbuf.at[pl.ds(0, NZL - 1)], z_r.at[0])
        for k in range(NZL - 1):
            total = total + zbuf[k]
        loads[2].wait()
        out_ref[...] = res_ref[...] + 0.5 * total

    keeps_q = c == zh

    @pl.when(jnp.logical_not(keeps_q))
    def _():
        give(0)

    p_multiply(ymod(-1))
    p_multiply(ymod(1))

    @pl.when(keeps_q)
    def _():
        take(0)

    p_step(3, (0, 1, 3, 2))
    for s in (2, 3):
        p_multiply(ymod(-s))
        p_multiply(ymod(s))
    for k in (0, 1, 3, 2):
        for direction in (0, 1):
            arrived(part(pbuf.at[opposite, xmod(-k)], direction), py_r.at[direction, NY // 2, k])
    p_multiply(opposite)

    @pl.when(keeps_q)
    def _():
        give(1)
        finish(0)

    @pl.when(jnp.logical_not(keeps_q))
    def _():
        take(1)
        finish(1)

    cnt_ref[0] = jnp.max(ranks[...])
    sent(raw.at[pl.ds(0, NY - 1)], raw_s.at[0])
    sent(raw_irr.at[pl.ds(0, NY - 1)], ri_s.at[0])
    sent(qbuf.at[0, 0], zx_s.at[0])
    sent(qbuf.at[0, pl.ds(0, NY - 1)], qy_s.at[0])
    sent(qbuf.at[pl.ds(0, NX - 1)], qx_s.at[0])
    sent(pbuf.at[0, pl.ds(0, NX - 1)], px_s.at[0])
    sent(pbuf.at[pl.ds(0, NY - 1)], py_s.at[0])
    sent(pair, pair_s.at[0])
    sent(zbuf.at[pl.ds(0, NZL - 1)], z_s.at[0])


def one_pass(amplitudes, integrals, start, row_irrep, cd_sizes, off):
    dma = pltpu.SemaphoreType.DMA
    hbm = pl.BlockSpec(memory_space=pltpu.HBM)
    vmem, smem = pl.BlockSpec(memory_space=pltpu.VMEM), pl.BlockSpec(memory_space=pltpu.SMEM)
    return pl.pallas_call(
        kernel,
        out_shape=(jax.ShapeDtypeStruct((RB, AB), F32), jax.ShapeDtypeStruct((1,), F32)),
        in_specs=[hbm] * 6,
        out_specs=(vmem, smem),
        scratch_shapes=[
            pltpu.VMEM((RW, NY * CH), F32),
            pltpu.VMEM((NY * CH, AB), F32),
            pltpu.VMEM((RB, AB), F32),
            pltpu.SMEM((RW,), jnp.int32),
            pltpu.SMEM((NIRR,), jnp.int32),
            pltpu.SMEM((1,), F32),
            pltpu.VMEM((NY, 3 * CH, AB), BF16),
            pltpu.VMEM((NY, CH), F32),
            pltpu.VMEM((8, RB), F32),
            pltpu.VMEM((NY, RW, CH), F32),
            pltpu.VMEM((NY, RB), F32),
            pltpu.VMEM((NX, NY, SLOTS, CH), F32),
            pltpu.VMEM((NY, NX, SLOTS, CH), F32),
            pltpu.VMEM((NZH, NX * RB, NX * SLOTS), BF16),
            pltpu.VMEM((NZH, NX * RB, RB), F32),
            pltpu.VMEM((2 * NX, RB), F32),
            pltpu.VMEM((NZH, NX * RB, AB), F32),
            pltpu.VMEM((NZL, RB, AB), F32),
            pltpu.VMEM((NZL - 1, RB, AB), F32),
            dma((6,)), dma((1,)), dma((1,)), dma((1,)), dma((1,)),
            dma((1,)), dma((NY,)), dma((1,)), dma((NY,)),
            dma((1,)), dma((2, 5, NX)), dma((1,)), dma((NX,)), dma((1,)), dma((1,)),
            dma((1,)), dma((NZL,)), dma((1,)), dma((1,)),
        ],
        compiler_params=pltpu.CompilerParams(
            collective_id=0, has_side_effects=True, vmem_limit_bytes=40 * 2**20
        ),
        name="ladder",
    )(amplitudes, integrals, start, row_irrep, cd_sizes, off)


def body(amplitudes, integrals, residual_in, row_irrep, cd_sizes):
    def run(start, off):
        return one_pass(amplitudes, integrals, start, row_irrep, cd_sizes, off)

    def more(state):
        _, top, off = state
        return top[0] >= off[0]

    def again(state):
        total, _, off = state
        total, top = run(total, off)
        return total, top, off + CAP

    zero = jnp.zeros((1,), F32)
    total, top = run(residual_in, zero)
    return lax.while_loop(more, again, (total, top, zero + CAP))[0]


def solution(mesh):
    in_specs = (P("wide", "narrow"), P("narrow", "wide"), P("narrow", "wide"), P("wide"), P())
    out_specs = P("narrow", "wide")
    return jax.shard_map(body, mesh=mesh, in_specs=in_specs, out_specs=out_specs, check_vma=False)
```

```python
import functools

import jax
import jax.numpy as jnp
from jax import lax
from jax.experimental import pallas as pl
from jax.experimental.pallas import tpu as pltpu
from jax.sharding import PartitionSpec as P

MESH = pl.DeviceIdType.MESH
F32 = jnp.float32
BF16 = jnp.bfloat16

NX, NZH, NY, NZL, NC = 4, 2, 8, 4, 2
RW = 16
RB = RW * NY
CH = 256
AB = 256
SLOTS = 32
CAP = SLOTS - 1
HALF = SLOTS // 2
COLS = CH // 2
PLACE = {0: 0, 1: 1, 7: 2, 2: 3, 6: 4, 3: 5, 5: 6, 4: 7}
RUNS = ((0, 3), (3, 5))
NIRR = 8


def split(value):
    high = value.astype(BF16)
    return high, (value - high.astype(F32)).astype(BF16)


def dot(a, b):
    return jnp.dot(a, b, preferred_element_type=F32)


def kernel(
    a_hbm, int_hbm, res_hbm, irr_hbm, sizes_hbm, off_hbm,
    out_ref, cnt_ref,
    a_ref, int_ref, res_ref, irr_ref, sizes_ref, off_ref, int3, ci_ref, irr_row, raw, raw_irr, qbuf, pbuf, sel, irr_col, ranks, acc, pair, zbuf,
    in_s, raw_s, raw_r, ri_s, ri_r, qy_s, qy_r, qx_s, qx_r, py_s, py_r, px_s, px_r, zx_s, zx_r,
    pair_s, pair_r, z_s, z_r,
):
    w, n = lax.axis_index("wide"), lax.axis_index("narrow")
    x, zh, y = w // (NZH * NY), (w // NY) % NZH, w % NY
    zl, c = n // NC, n % NC

    def dev(x_, zh_, y_, zl_, c_):
        return (x_ * (NZH * NY) + zh_ * NY + y_, zl_ * NC + c_)

    ymod = lambda k: lax.rem(y + (k + NY), NY)
    xmod = lambda k: lax.rem(x + (k + NX), NX)
    partner = dev(x, zh, y, zl, 1 - c)
    up, down = dev(x, zh, ymod(1), zl, c), dev(x, zh, ymod(-1), zl, c)
    y_peers = [dev(x, zh, ymod(k), zl, c) for k in range(1, NY)]
    across = dev(x, 1 - zh, y, zl, c)
    x_peers = [dev(xmod(k), zh, y, zl, c) for k in range(1, NX)]
    z_peers = [dev(x, zh, y, lax.rem(zl + k, NZL), c) for k in range(1, NZL)]

    barrier = pltpu.get_barrier_semaphore()
    everyone = y_peers + x_peers + z_peers + [partner, across]
    for peer in everyone:
        pl.semaphore_signal(barrier, inc=1, device_id=peer, device_id_type=MESH)

    loads = [
        pltpu.make_async_copy(src, dst, in_s.at[i])
        for i, (src, dst) in enumerate((
            (a_hbm, a_ref), (int_hbm, int_ref), (res_hbm, res_ref),
            (irr_hbm, irr_ref), (sizes_hbm, sizes_ref), (off_hbm, off_ref),
        ))
    ]
    for load in loads:
        load.start()
    for load in loads[3:]:
        load.wait()
    lane = lax.broadcasted_iota(jnp.int32, (8, 128), 1)
    row = jnp.zeros((8, 128), F32)
    for r in range(RW):
        row = jnp.where(lane == y * RW + r, irr_ref[r].astype(F32), row)
    irr_row[...] = row
    cd = (
        n * (NY * CH)
        + CH * lax.broadcasted_iota(jnp.int32, (NY, CH), 0)
        + lax.broadcasted_iota(jnp.int32, (NY, CH), 1)
    )
    end = jnp.int32(0)
    col = jnp.zeros((NY, CH), F32)
    for i in range(NIRR):
        end = end + sizes_ref[i]
        col = col + jnp.where(cd >= end, 1.0, 0.0)
    ci_ref[...] = col
    off = off_ref[0]

    def send(src, dst, s, r, to):
        copy = pltpu.make_async_remote_copy(
            src_ref=src, dst_ref=dst, send_sem=s, recv_sem=r, device_id=to, device_id_type=MESH
        )
        copy.start()

    def sent(total, s):
        pltpu.make_async_remote_copy(
            src_ref=total, dst_ref=total, send_sem=s, recv_sem=s, device_id=partner, device_id_type=MESH
        ).wait_send()

    def arrived(dst, r):
        pltpu.make_async_remote_copy(
            src_ref=dst, dst_ref=dst, send_sem=r, recv_sem=r, device_id=partner, device_id_type=MESH
        ).wait_recv()

    chunk = lambda j: pl.ds(pl.multiple_of(j * CH, CH), CH)

    def split_integrals(j, _):
        high, low = split(int_ref[chunk(j), :])
        int3[j, 0:CH] = high
        int3[j, CH:2 * CH] = high
        int3[j, 2 * CH:] = low
        return 0

    loads[0].wait()
    pl.semaphore_wait(barrier, len(everyone))

    for k in (4, 3, 5, 2, 6, 1, 7):
        to = y_peers[k - 1]
        send(irr_row.at[pl.ds(0, 1)], raw_irr.at[pl.ds(y, 1)], ri_s.at[0], ri_r.at[0], to)
        send(a_ref.at[:, chunk(ymod(k))], raw.at[y], raw_s.at[0], raw_r.at[0], to)
    raw[y] = a_ref[:, chunk(y)]
    raw_irr[pl.ds(y, 1), :] = row[0:1]
    loads[1].wait()
    lax.fori_loop(0, NY, split_integrals, 0)

    sub_i = lax.broadcasted_iota(jnp.int32, (RB, RB), 0)
    lane_i = lax.broadcasted_iota(jnp.int32, (RB, RB), 1)

    def ranks_of(irr_lane):
        along_lane = jnp.broadcast_to(irr_lane, (RB, RB))
        along_sub = along_lane.T
        same = along_lane == along_sub
        rank_lane = jnp.sum(jnp.where(same & (sub_i < lane_i), 1.0, 0.0), axis=0, keepdims=True)
        rank_sub = jnp.sum(jnp.where(same & (lane_i < sub_i), 1.0, 0.0), axis=1, keepdims=True)
        return along_sub, rank_lane, rank_sub

    def pack():
        irr_lane = jnp.sum(raw_irr[...], axis=0, keepdims=True)
        along_sub, rank_lane, _ = ranks_of(irr_lane)
        slot = lax.broadcasted_iota(jnp.int32, (SLOTS, RB), 0).astype(F32)
        pick = jnp.where((rank_lane - off == slot) & (slot < CAP), 1.0, 0.0).astype(BF16)
        here = ci_ref[pl.ds(y, 1), :]
        keep = jnp.concatenate([along_sub, along_sub], axis=1) == here
        masked = jnp.where(keep, raw[...].reshape(RB, CH), 0.0)
        high = masked.astype(BF16)
        rest = masked - high.astype(F32)
        mid, low = split(rest)
        packed = dot(pick, high) + dot(pick, mid) + dot(pick, low)
        last = lax.broadcasted_iota(jnp.int32, (SLOTS, CH), 0) == CAP
        tail = jnp.concatenate([irr_lane, jnp.zeros((1, CH - RB), F32)], axis=1)
        packed = jnp.where(last, jnp.broadcast_to(tail, (SLOTS, CH)), packed)
        pbuf[0, y, 0] = packed[:, :COLS]
        qbuf[0, 0, 0] = packed[:, COLS:]

    def open_blocks(g, srcs):
        for k, src in enumerate(srcs):
            irr_lane = src[pl.ds(CAP, 1), 0:RB]
            along_sub, rank_lane, rank_sub = ranks_of(irr_lane)
            slot = lax.broadcasted_iota(jnp.int32, (RB, NX * SLOTS), 1) - k * SLOTS
            pick = (rank_sub - off == slot.astype(F32)) & (slot >= 0) & (slot < CAP)
            sel[g, k * RB:(k + 1) * RB, :] = jnp.where(pick, 1.0, 0.0).astype(BF16)
            irr_col[g, k * RB:(k + 1) * RB, :] = along_sub
            ranks[pl.ds(NX * g + k, 1), :] = rank_lane

    def multiply(g, slot, first=False):
        j, rows = ymod(-slot), (NX * SLOTS, COLS)
        both = jnp.concatenate([pbuf[g, j].reshape(rows), qbuf[g, :, PLACE[slot]].reshape(rows)], axis=1)
        high, low = split(both)
        spread = dot(sel[g], jnp.concatenate([high, low], axis=1))
        keep = jnp.concatenate([irr_col[g], irr_col[g]], axis=1) == ci_ref[pl.ds(j, 1), :]
        e_hi = jnp.where(keep, spread[:, :CH], 0.0).astype(BF16)
        e_lo = jnp.where(keep, spread[:, CH:], 0.0).astype(BF16)
        term = dot(jnp.concatenate([e_hi, e_lo, e_hi], axis=1), int3[j])
        if first:
            acc[g] = term
        else:
            acc[g] += term

    arrived(raw_irr.at[pl.ds(0, NY - 1)], ri_r.at[0])
    arrived(raw.at[pl.ds(0, NY - 1)], raw_r.at[0])
    pack()

    def q_start(g):
        for k in (1, 7, 2, 6, 3, 5, 4):
            send(qbuf.at[g, 0, 0], qbuf.at[g, 0, PLACE[k]], qy_s.at[0], qy_r.at[g, int(PLACE[k] > 2)], y_peers[k - 1])

    def q_along_x(g, run):
        at, count = RUNS[run]
        come = pl.ds(max(at, 1), count - (run == 0))
        arrived(qbuf.at[g, 0, come], qy_r.at[g, run])
        for k in (2, 1, 3):
            send(
                qbuf.at[g, 0, pl.ds(at, count)], qbuf.at[g, k, pl.ds(at, count)],
                qx_s.at[0], qx_r.at[g, run], x_peers[k - 1],
            )

    def q_here(g, run):
        at, count = RUNS[run]
        arrived(qbuf.at[g, pl.ds(1, NX - 1), pl.ds(at, count)], qx_r.at[g, run])

    def p_part(g, j, group, s, direction):
        which = pl.ds(0, 1) if group == 0 else pl.ds(1, NX - 1)
        if s == NY // 2:
            return pbuf.at[g, j, which, pl.ds(direction * HALF, HALF)]
        return pbuf.at[g, j, which]

    def p_along_y(g, j, group, s, direction):
        ref = p_part(g, j, group, s, direction)
        send(ref, ref, py_s.at[0], py_r.at[g, direction, s, group], (up, down)[direction])

    def p_start(g):
        for k in (2, 1, 3):
            send(pbuf.at[g, y, 0], pbuf.at[g, y, k], px_s.at[0], px_r.at[g], x_peers[k - 1])
        for direction in (0, 1):
            p_along_y(g, y, 0, 1, direction)

    def p_x(g):
        arrived(pbuf.at[g, y, pl.ds(1, NX - 1)], px_r.at[g])
        for direction in (0, 1):
            p_along_y(g, y, 1, 1, direction)

    def p_step(g, s, group):
        for direction, j in ((0, ymod(-s)), (1, ymod(s))):
            arrived(p_part(g, j, group, s, direction), py_r.at[g, direction, s, group])
            p_along_y(g, j, group, s + 1, direction)

    opposite = ymod(NY // 2)

    def p_last(g):
        for group in (0, 1):
            for direction in (0, 1):
                arrived(p_part(g, opposite, group, NY // 2, direction), py_r.at[g, direction, NY // 2, group])

    def use(g, *slots):
        for slot in slots:
            if slot == 0:
                open_blocks(g, [pbuf.at[g, y, k] for k in range(NX)])
            multiply(g, slot, slot == 0)

    send(pbuf.at[0, y, 0], pbuf.at[1, y, 0], zx_s.at[0], zx_r.at[0], across)
    send(qbuf.at[0, 0, 0], qbuf.at[1, 0, 0], zx_s.at[0], zx_r.at[1], across)
    p_start(0)
    q_start(0)
    q_along_x(0, 0)
    p_step(0, 1, 0)
    p_x(0)
    arrived(pbuf.at[1, y, 0], zx_r.at[0])
    p_start(1)
    arrived(qbuf.at[1, 0, 0], zx_r.at[1])
    q_start(1)
    p_step(0, 2, 0)
    q_along_x(0, 1)
    p_step(0, 1, 1)
    q_here(0, 0)
    use(0, 0)
    p_step(0, 3, 0)
    q_along_x(1, 0)
    p_step(1, 1, 0)
    p_step(0, 2, 1)
    p_x(1)
    use(0, 1, 7)
    p_step(1, 2, 0)
    q_along_x(1, 1)
    p_step(0, 3, 1)
    p_step(1, 1, 1)
    q_here(0, 1)
    use(0, 2, 6)
    q_here(1, 0)
    use(1, 0)
    p_step(1, 3, 0)
    use(0, 3, 5)
    p_step(1, 2, 1)
    p_last(0)
    use(0, 4)

    block = lambda d: pl.ds(pl.multiple_of(xmod(-d) * RB, RB), RB)

    def pair_copy(g, d):
        return pltpu.make_async_remote_copy(
            src_ref=acc.at[g, block(d)], dst_ref=pair.at[d], send_sem=pair_s.at[0], recv_sem=pair_r.at[d],
            device_id=partner, device_id_type=MESH,
        )

    def z_copy(g, d):
        slot = lax.rem(zl - d + NZL, NZL) - 1
        return pltpu.make_async_remote_copy(
            src_ref=acc.at[g, block(d)], dst_ref=zbuf.at[slot], send_sem=z_s.at[0], recv_sem=z_r.at[0],
            device_id=dev(x, zh, y, d, c), device_id_type=MESH,
        )

    def nth(t):
        return jnp.where(zl < NZL // 2, NZL - 1 - t, t)

    def give(g):
        def one(t, _):
            pair_copy(g, nth(t)).start()
            return 0

        lax.fori_loop(0, NZL, one, 0)

    def take(g):
        def one(t, _):
            d = nth(t)
            arrived(pair.at[d], pair_r.at[d])
            acc[g, block(d)] += pair[d]

            @pl.when(d != zl)
            def _():
                z_copy(g, d).start()

            return 0

        lax.fori_loop(0, NZL, one, 0)

    def finish(g):
        total = acc[g, block(zl)]
        arrived(zbuf.at[pl.ds(0, NZL - 1)], z_r.at[0])
        for k in range(NZL - 1):
            total = total + zbuf[k]
        loads[2].wait()
        out_ref[...] = res_ref[...] + 0.5 * total

    keeps_own = c == zh

    @pl.when(jnp.logical_not(keeps_own))
    def _():
        give(0)

    use(1, 1, 7)

    @pl.when(keeps_own)
    def _():
        take(0)

    p_step(1, 3, 1)
    q_here(1, 1)
    use(1, 2, 6, 3, 5)
    p_last(1)
    use(1, 4)

    @pl.when(keeps_own)
    def _():
        give(1)
        finish(0)

    @pl.when(jnp.logical_not(keeps_own))
    def _():
        take(1)
        finish(1)

    cnt_ref[0] = jnp.max(ranks[...])
    sent(raw.at[pl.ds(0, NY - 1)], raw_s.at[0])
    sent(raw_irr.at[pl.ds(0, NY - 1)], ri_s.at[0])
    sent(pbuf.at[0, 0, pl.ds(0, 2)], zx_s.at[0])
    sent(qbuf.at[:, 0, pl.ds(0, NY - 1)], qy_s.at[0])
    sent(qbuf.at[:, pl.ds(0, NX - 1)], qx_s.at[0])
    sent(pbuf.at[:, 0, pl.ds(0, NX - 1)], px_s.at[0])
    sent(pbuf.at[:, pl.ds(0, NY - 1)], py_s.at[0])
    sent(pair, pair_s.at[0])
    sent(zbuf.at[pl.ds(0, NZL - 1)], z_s.at[0])


def one_pass(amplitudes, integrals, start, row_irrep, cd_sizes, off):
    dma = pltpu.SemaphoreType.DMA
    hbm = pl.BlockSpec(memory_space=pltpu.HBM)
    vmem, smem = pl.BlockSpec(memory_space=pltpu.VMEM), pl.BlockSpec(memory_space=pltpu.SMEM)
    return pl.pallas_call(
        kernel,
        out_shape=(jax.ShapeDtypeStruct((RB, AB), F32), jax.ShapeDtypeStruct((1,), F32)),
        in_specs=[hbm] * 6,
        out_specs=(vmem, smem),
        scratch_shapes=[
            pltpu.VMEM((RW, NY * CH), F32),
            pltpu.VMEM((NY * CH, AB), F32),
            pltpu.VMEM((RB, AB), F32),
            pltpu.SMEM((RW,), jnp.int32),
            pltpu.SMEM((NIRR,), jnp.int32),
            pltpu.SMEM((1,), F32),
            pltpu.VMEM((NY, 3 * CH, AB), BF16),
            pltpu.VMEM((NY, CH), F32),
            pltpu.VMEM((8, RB), F32),
            pltpu.VMEM((NY, RW, CH), F32),
            pltpu.VMEM((NY, RB), F32),
            pltpu.VMEM((NZH, NX, NY, SLOTS, COLS), F32),
            pltpu.VMEM((NZH, NY, NX, SLOTS, COLS), F32),
            pltpu.VMEM((NZH, NX * RB, NX * SLOTS), BF16),
            pltpu.VMEM((NZH, NX * RB, RB), F32),
            pltpu.VMEM((2 * NX, RB), F32),
            pltpu.VMEM((NZH, NX * RB, AB), F32),
            pltpu.VMEM((NZL, RB, AB), F32),
            pltpu.VMEM((NZL - 1, RB, AB), F32),
            dma((6,)), dma((1,)), dma((1,)), dma((1,)), dma((1,)),
            dma((1,)), dma((NZH, 2)), dma((1,)), dma((NZH, 2)),
            dma((1,)), dma((NZH, 2, 5, 2)), dma((1,)), dma((NZH,)), dma((1,)), dma((2,)),
            dma((1,)), dma((NZL,)), dma((1,)), dma((1,)),
        ],
        compiler_params=pltpu.CompilerParams(
            collective_id=0, has_side_effects=True, vmem_limit_bytes=40 * 2**20
        ),
        name="ladder",
    )(amplitudes, integrals, start, row_irrep, cd_sizes, off)


def body(amplitudes, integrals, residual_in, row_irrep, cd_sizes):
    def run(start, off):
        return one_pass(amplitudes, integrals, start, row_irrep, cd_sizes, off)

    def more(state):
        _, top, off = state
        return top[0] >= off[0]

    def again(state):
        total, _, off = state
        total, top = run(total, off)
        return total, top, off + CAP

    zero = jnp.zeros((1,), F32)
    total, top = run(residual_in, zero)
    return lax.while_loop(more, again, (total, top, zero + CAP))[0]


def solution(mesh):
    in_specs = (P("wide", "narrow"), P("narrow", "wide"), P("narrow", "wide"), P("wide"), P())
    out_specs = P("narrow", "wide")
    return jax.shard_map(body, mesh=mesh, in_specs=in_specs, out_specs=out_specs, check_vma=False)
```

```python
import functools

import jax
import jax.numpy as jnp
from jax import lax
from jax.experimental import pallas as pl
from jax.experimental.pallas import tpu as pltpu
from jax.sharding import PartitionSpec as P

MESH = pl.DeviceIdType.MESH
F32 = jnp.float32
BF16 = jnp.bfloat16

NX, NZH, NY, NZL, NC = 4, 2, 8, 4, 2
RW = 16
RB = RW * NY
CH = 256
AB = 256
SLOTS = 32
CAP = SLOTS - 1
HALF = SLOTS // 2
COLS = CH // 2
PLACE = {0: 0, 1: 1, 7: 2, 2: 3, 6: 4, 3: 5, 5: 6, 4: 7}
RUNS = ((0, 3), (3, 5))
NIRR = 8


def split(value):
    high = value.astype(BF16)
    return high, (value - high.astype(F32)).astype(BF16)


def dot(a, b):
    return jnp.dot(a, b, preferred_element_type=F32)


def kernel(
    a_hbm, int_hbm, res_hbm, irr_hbm, sizes_hbm, off_hbm,
    out_ref, cnt_ref,
    a_ref, int_ref, res_ref, irr_ref, sizes_ref, off_ref, int3, ci_ref, irr_row, raw, raw_irr, qbuf, pbuf, sel, irr_col, ranks, acc, pair, zbuf,
    in_s, raw_s, raw_r, ri_s, ri_r, qy_s, qy_r, qx_s, qx_r, py_s, py_r, px_s, px_r, zx_s, zx_r,
    pair_s, pair_r, z_s, z_r,
):
    w, n = lax.axis_index("wide"), lax.axis_index("narrow")
    x, zh, y = w // (NZH * NY), (w // NY) % NZH, w % NY
    zl, c = n // NC, n % NC

    def dev(x_, zh_, y_, zl_, c_):
        return (x_ * (NZH * NY) + zh_ * NY + y_, zl_ * NC + c_)

    ymod = lambda k: lax.rem(y + (k + NY), NY)
    xmod = lambda k: lax.rem(x + (k + NX), NX)
    partner = dev(x, zh, y, zl, 1 - c)
    up, down = dev(x, zh, ymod(1), zl, c), dev(x, zh, ymod(-1), zl, c)
    y_peers = [dev(x, zh, ymod(k), zl, c) for k in range(1, NY)]
    across = dev(x, 1 - zh, y, zl, c)
    x_peers = [dev(xmod(k), zh, y, zl, c) for k in range(1, NX)]
    z_peers = [dev(x, zh, y, lax.rem(zl + k, NZL), c) for k in range(1, NZL)]

    barrier = pltpu.get_barrier_semaphore()
    everyone = y_peers + x_peers + z_peers + [partner, across]
    for peer in everyone:
        pl.semaphore_signal(barrier, inc=1, device_id=peer, device_id_type=MESH)

    loads = [
        pltpu.make_async_copy(src, dst, in_s.at[i])
        for i, (src, dst) in enumerate((
            (a_hbm, a_ref), (int_hbm, int_ref), (res_hbm, res_ref),
            (irr_hbm, irr_ref), (sizes_hbm, sizes_ref), (off_hbm, off_ref),
        ))
    ]
    for load in loads:
        load.start()
    for load in loads[3:]:
        load.wait()
    lane = lax.broadcasted_iota(jnp.int32, (8, 128), 1)
    row = jnp.zeros((8, 128), F32)
    for r in range(RW):
        row = jnp.where(lane == y * RW + r, irr_ref[r].astype(F32), row)
    irr_row[...] = row
    cd = (
        n * (NY * CH)
        + CH * lax.broadcasted_iota(jnp.int32, (NY, CH), 0)
        + lax.broadcasted_iota(jnp.int32, (NY, CH), 1)
    )
    end = jnp.int32(0)
    col = jnp.zeros((NY, CH), F32)
    for i in range(NIRR):
        end = end + sizes_ref[i]
        col = col + jnp.where(cd >= end, 1.0, 0.0)
    ci_ref[...] = col
    off = off_ref[0]

    def send(src, dst, s, r, to):
        copy = pltpu.make_async_remote_copy(
            src_ref=src, dst_ref=dst, send_sem=s, recv_sem=r, device_id=to, device_id_type=MESH
        )
        copy.start()

    def sent(total, s):
        pltpu.make_async_remote_copy(
            src_ref=total, dst_ref=total, send_sem=s, recv_sem=s, device_id=partner, device_id_type=MESH
        ).wait_send()

    def arrived(dst, r):
        pltpu.make_async_remote_copy(
            src_ref=dst, dst_ref=dst, send_sem=r, recv_sem=r, device_id=partner, device_id_type=MESH
        ).wait_recv()

    chunk = lambda j: pl.ds(pl.multiple_of(j * CH, CH), CH)

    def split_integrals(j, _):
        high, low = split(int_ref[chunk(j), :])
        int3[j, 0:CH] = high
        int3[j, CH:2 * CH] = high
        int3[j, 2 * CH:] = low
        return 0

    loads[0].wait()
    pl.semaphore_wait(barrier, len(everyone))

    for k in (4, 3, 5, 2, 6, 1, 7):
        to = y_peers[k - 1]
        send(irr_row.at[pl.ds(0, 1)], raw_irr.at[pl.ds(y, 1)], ri_s.at[0], ri_r.at[0], to)
        send(a_ref.at[:, chunk(ymod(k))], raw.at[y], raw_s.at[0], raw_r.at[0], to)
    raw[y] = a_ref[:, chunk(y)]
    raw_irr[pl.ds(y, 1), :] = row[0:1]
    loads[1].wait()
    lax.fori_loop(0, NY, split_integrals, 0)

    sub_i = lax.broadcasted_iota(jnp.int32, (RB, RB), 0)
    lane_i = lax.broadcasted_iota(jnp.int32, (RB, RB), 1)

    def ranks_of(irr_lane):
        along_lane = jnp.broadcast_to(irr_lane, (RB, RB))
        along_sub = along_lane.T
        same = along_lane == along_sub
        rank_lane = jnp.sum(jnp.where(same & (sub_i < lane_i), 1.0, 0.0), axis=0, keepdims=True)
        rank_sub = jnp.sum(jnp.where(same & (lane_i < sub_i), 1.0, 0.0), axis=1, keepdims=True)
        return along_sub, rank_lane, rank_sub

    def pack():
        irr_lane = jnp.sum(raw_irr[...], axis=0, keepdims=True)
        along_sub, rank_lane, _ = ranks_of(irr_lane)
        slot = lax.broadcasted_iota(jnp.int32, (SLOTS, RB), 0).astype(F32)
        pick = jnp.where((rank_lane - off == slot) & (slot < CAP), 1.0, 0.0).astype(BF16)
        here = ci_ref[pl.ds(y, 1), :]
        keep = jnp.concatenate([along_sub, along_sub], axis=1) == here
        masked = jnp.where(keep, raw[...].reshape(RB, CH), 0.0)
        high = masked.astype(BF16)
        rest = masked - high.astype(F32)
        mid, low = split(rest)
        packed = dot(pick, high) + dot(pick, mid) + dot(pick, low)
        last = lax.broadcasted_iota(jnp.int32, (SLOTS, CH), 0) == CAP
        tail = jnp.concatenate([irr_lane, jnp.zeros((1, CH - RB), F32)], axis=1)
        packed = jnp.where(last, jnp.broadcast_to(tail, (SLOTS, CH)), packed)
        pbuf[0, y, 0] = packed[:, :COLS]
        qbuf[0, 0, 0] = packed[:, COLS:]

    def open_blocks(g, srcs):
        for k, src in enumerate(srcs):
            irr_lane = src[pl.ds(CAP, 1), 0:RB]
            along_sub, rank_lane, rank_sub = ranks_of(irr_lane)
            slot = lax.broadcasted_iota(jnp.int32, (RB, NX * SLOTS), 1) - k * SLOTS
            pick = (rank_sub - off == slot.astype(F32)) & (slot >= 0) & (slot < CAP)
            sel[g, k * RB:(k + 1) * RB, :] = jnp.where(pick, 1.0, 0.0).astype(BF16)
            irr_col[g, k * RB:(k + 1) * RB, :] = along_sub
            ranks[pl.ds(NX * g + k, 1), :] = rank_lane

    def multiply(g, slot, first=False):
        j, rows = ymod(-slot), (NX * SLOTS, COLS)
        both = jnp.concatenate([pbuf[g, j].reshape(rows), qbuf[g, :, PLACE[slot]].reshape(rows)], axis=1)
        high, low = split(both)
        spread = dot(sel[g], jnp.concatenate([high, low], axis=1))
        keep = jnp.concatenate([irr_col[g], irr_col[g]], axis=1) == ci_ref[pl.ds(j, 1), :]
        e_hi = jnp.where(keep, spread[:, :CH], 0.0).astype(BF16)
        e_lo = jnp.where(keep, spread[:, CH:], 0.0).astype(BF16)
        term = dot(jnp.concatenate([e_hi, e_lo, e_hi], axis=1), int3[j])
        if first:
            acc[g] = term
        else:
            acc[g] += term

    arrived(raw_irr.at[pl.ds(0, NY - 1)], ri_r.at[0])
    arrived(raw.at[pl.ds(0, NY - 1)], raw_r.at[0])
    pack()

    def q_start(g):
        for k in (1, 7, 2, 6, 3, 5, 4):
            send(qbuf.at[g, 0, 0], qbuf.at[g, 0, PLACE[k]], qy_s.at[0], qy_r.at[g, int(PLACE[k] > 2)], y_peers[k - 1])

    def q_along_x(g, run):
        at, count = RUNS[run]
        come = pl.ds(max(at, 1), count - (run == 0))
        arrived(qbuf.at[g, 0, come], qy_r.at[g, run])
        for k in (2, 1, 3):
            send(
                qbuf.at[g, 0, pl.ds(at, count)], qbuf.at[g, k, pl.ds(at, count)],
                qx_s.at[0], qx_r.at[g, run], x_peers[k - 1],
            )

    def q_here(g, run):
        at, count = RUNS[run]
        arrived(qbuf.at[g, pl.ds(1, NX - 1), pl.ds(at, count)], qx_r.at[g, run])

    def p_part(g, j, group, s, direction):
        which = pl.ds(0, 1) if group == 0 else pl.ds(1, NX - 1)
        if s == NY // 2:
            return pbuf.at[g, j, which, pl.ds(direction * HALF, HALF)]
        return pbuf.at[g, j, which]

    def p_along_y(g, j, group, s, direction):
        ref = p_part(g, j, group, s, direction)
        send(ref, ref, py_s.at[0], py_r.at[g, direction, s, group], (up, down)[direction])

    def p_start(g):
        for k in (2, 1, 3):
            send(pbuf.at[g, y, 0], pbuf.at[g, y, k], px_s.at[0], px_r.at[g], x_peers[k - 1])
        for direction in (0, 1):
            p_along_y(g, y, 0, 1, direction)

    def p_x(g):
        arrived(pbuf.at[g, y, pl.ds(1, NX - 1)], px_r.at[g])
        for direction in (0, 1):
            p_along_y(g, y, 1, 1, direction)

    def p_step(g, s, group):
        for direction, j in ((0, ymod(-s)), (1, ymod(s))):
            arrived(p_part(g, j, group, s, direction), py_r.at[g, direction, s, group])
            p_along_y(g, j, group, s + 1, direction)

    opposite = ymod(NY // 2)

    def p_last(g):
        for group in (0, 1):
            for direction in (0, 1):
                arrived(p_part(g, opposite, group, NY // 2, direction), py_r.at[g, direction, NY // 2, group])

    def use(g, *slots):
        for slot in slots:
            if slot == 0:
                open_blocks(g, [pbuf.at[g, y, k] for k in range(NX)])
            multiply(g, slot, slot == 0)

    send(pbuf.at[0, y, 0], pbuf.at[1, y, 0], zx_s.at[0], zx_r.at[0], across)
    send(qbuf.at[0, 0, 0], qbuf.at[1, 0, 0], zx_s.at[0], zx_r.at[1], across)
    p_start(0)
    q_start(0)
    q_along_x(0, 0)
    p_step(0, 1, 0)
    p_x(0)
    arrived(pbuf.at[1, y, 0], zx_r.at[0])
    p_start(1)
    arrived(qbuf.at[1, 0, 0], zx_r.at[1])
    q_start(1)
    p_step(0, 2, 0)
    q_along_x(0, 1)
    p_step(0, 1, 1)
    q_here(0, 0)
    use(0, 0)
    p_step(0, 3, 0)
    q_along_x(1, 0)
    p_step(1, 1, 0)
    p_step(0, 2, 1)
    p_x(1)
    use(0, 1, 7)
    p_step(1, 2, 0)
    q_along_x(1, 1)
    p_step(0, 3, 1)
    p_step(1, 1, 1)
    q_here(0, 1)
    use(0, 2, 6)
    q_here(1, 0)
    use(1, 0)
    p_step(1, 3, 0)
    use(0, 3, 5)
    p_step(1, 2, 1)
    p_last(0)
    use(0, 4)

    block = lambda d: pl.ds(pl.multiple_of(xmod(-d) * RB, RB), RB)

    def pair_copy(g, d):
        return pltpu.make_async_remote_copy(
            src_ref=acc.at[g, block(d)], dst_ref=pair.at[d], send_sem=pair_s.at[0], recv_sem=pair_r.at[d],
            device_id=partner, device_id_type=MESH,
        )

    def z_copy(g, d):
        slot = lax.rem(zl - d + NZL, NZL) - 1
        return pltpu.make_async_remote_copy(
            src_ref=acc.at[g, block(d)], dst_ref=zbuf.at[slot], send_sem=z_s.at[0], recv_sem=z_r.at[0],
            device_id=dev(x, zh, y, d, c), device_id_type=MESH,
        )

    def nth(t):
        return jnp.where(zl < NZL // 2, NZL - 1 - t, t)

    def give(g):
        def one(t, _):
            pair_copy(g, nth(t)).start()
            return 0

        lax.fori_loop(0, NZL, one, 0)

    def take(g):
        def one(t, _):
            d = nth(t)
            arrived(pair.at[d], pair_r.at[d])
            acc[g, block(d)] += pair[d]

            @pl.when(d != zl)
            def _():
                z_copy(g, d).start()

            return 0

        lax.fori_loop(0, NZL, one, 0)

    def finish(g):
        total = acc[g, block(zl)]
        arrived(zbuf.at[pl.ds(0, NZL - 1)], z_r.at[0])
        for k in range(NZL - 1):
            total = total + zbuf[k]
        loads[2].wait()
        out_ref[...] = res_ref[...] + 0.5 * total

    keeps_own = c == zh

    @pl.when(jnp.logical_not(keeps_own))
    def _():
        give(0)

    @pl.when(keeps_own)
    def _():
        take(0)

    use(1, 1, 7)

    p_step(1, 3, 1)
    q_here(1, 1)
    use(1, 2, 6, 3, 5)
    p_last(1)
    use(1, 4)

    @pl.when(keeps_own)
    def _():
        give(1)
        finish(0)

    @pl.when(jnp.logical_not(keeps_own))
    def _():
        take(1)
        finish(1)

    cnt_ref[0] = jnp.max(ranks[...])
    sent(raw.at[pl.ds(0, NY - 1)], raw_s.at[0])
    sent(raw_irr.at[pl.ds(0, NY - 1)], ri_s.at[0])
    sent(pbuf.at[0, 0, pl.ds(0, 2)], zx_s.at[0])
    sent(qbuf.at[:, 0, pl.ds(0, NY - 1)], qy_s.at[0])
    sent(qbuf.at[:, pl.ds(0, NX - 1)], qx_s.at[0])
    sent(pbuf.at[:, 0, pl.ds(0, NX - 1)], px_s.at[0])
    sent(pbuf.at[:, pl.ds(0, NY - 1)], py_s.at[0])
    sent(pair, pair_s.at[0])
    sent(zbuf.at[pl.ds(0, NZL - 1)], z_s.at[0])


def one_pass(amplitudes, integrals, start, row_irrep, cd_sizes, off):
    dma = pltpu.SemaphoreType.DMA
    hbm = pl.BlockSpec(memory_space=pltpu.HBM)
    vmem, smem = pl.BlockSpec(memory_space=pltpu.VMEM), pl.BlockSpec(memory_space=pltpu.SMEM)
    return pl.pallas_call(
        kernel,
        out_shape=(jax.ShapeDtypeStruct((RB, AB), F32), jax.ShapeDtypeStruct((1,), F32)),
        in_specs=[hbm] * 6,
        out_specs=(vmem, smem),
        scratch_shapes=[
            pltpu.VMEM((RW, NY * CH), F32),
            pltpu.VMEM((NY * CH, AB), F32),
            pltpu.VMEM((RB, AB), F32),
            pltpu.SMEM((RW,), jnp.int32),
            pltpu.SMEM((NIRR,), jnp.int32),
            pltpu.SMEM((1,), F32),
            pltpu.VMEM((NY, 3 * CH, AB), BF16),
            pltpu.VMEM((NY, CH), F32),
            pltpu.VMEM((8, RB), F32),
            pltpu.VMEM((NY, RW, CH), F32),
            pltpu.VMEM((NY, RB), F32),
            pltpu.VMEM((NZH, NX, NY, SLOTS, COLS), F32),
            pltpu.VMEM((NZH, NY, NX, SLOTS, COLS), F32),
            pltpu.VMEM((NZH, NX * RB, NX * SLOTS), BF16),
            pltpu.VMEM((NZH, NX * RB, RB), F32),
            pltpu.VMEM((2 * NX, RB), F32),
            pltpu.VMEM((NZH, NX * RB, AB), F32),
            pltpu.VMEM((NZL, RB, AB), F32),
            pltpu.VMEM((NZL - 1, RB, AB), F32),
            dma((6,)), dma((1,)), dma((1,)), dma((1,)), dma((1,)),
            dma((1,)), dma((NZH, 2)), dma((1,)), dma((NZH, 2)),
            dma((1,)), dma((NZH, 2, 5, 2)), dma((1,)), dma((NZH,)), dma((1,)), dma((2,)),
            dma((1,)), dma((NZL,)), dma((1,)), dma((1,)),
        ],
        compiler_params=pltpu.CompilerParams(
            collective_id=0, has_side_effects=True, vmem_limit_bytes=40 * 2**20
        ),
        name="ladder",
    )(amplitudes, integrals, start, row_irrep, cd_sizes, off)


def body(amplitudes, integrals, residual_in, row_irrep, cd_sizes):
    def run(start, off):
        return one_pass(amplitudes, integrals, start, row_irrep, cd_sizes, off)

    def more(state):
        _, top, off = state
        return top[0] >= off[0]

    def again(state):
        total, _, off = state
        total, top = run(total, off)
        return total, top, off + CAP

    zero = jnp.zeros((1,), F32)
    total, top = run(residual_in, zero)
    return lax.while_loop(more, again, (total, top, zero + CAP))[0]


def solution(mesh):
    in_specs = (P("wide", "narrow"), P("narrow", "wide"), P("narrow", "wide"), P("wide"), P())
    out_specs = P("narrow", "wide")
    return jax.shard_map(body, mesh=mesh, in_specs=in_specs, out_specs=out_specs, check_vma=False)
```
